128 devices in a mesh: ctx: 16 (over y, x), shard: 8 (over z, core).
Axes of the slice: x: 4, y: 4, z: 4, core: 2. Of those that a mesh axis runs over, the one named last changes fastest.
Arguments:
- queries: bfloat16 [4096, 12288], P('ctx', 'shard'), may hold values from -150 to 150
- latent_keys: bfloat16 [4096, 576], P('ctx'), may hold values from -8 to 8
- up_keys: bfloat16 [64, 128, 512], P('shard', 'ctx'), may hold values from -0.5 to 0.5
- up_values: bfloat16 [64, 512, 128], P('shard', 'ctx'), may hold values from -0.25 to 0.25
- out_weight: bfloat16 [64, 128, 7168], P('shard', None, 'ctx'), may hold values from -0.1875 to 0.1875
- keys_scale: int32 [64, 4], replicated, may hold values from -1 to 1
- values_scale: int32 [64, 4], replicated, may hold values from -1 to 1
- out_scale: int32 [64, 56], replicated, may hold values from -1 to 1
Outputs:
- mixed: bfloat16 [4096, 7168], P('ctx', 'shard')
The draws below stay inside these ranges and needn't reach their ends.
All inputs are finite; a program needn't handle non-finite values.
Results may differ from the reference program's by a relative error of at most 0.019.
Values may be sent and summed in bfloat16 or wider, within the bound.
A program may use at most 192 MiB of HBM per device.

```python
import jax
import jax.numpy as jnp
from jax import lax

D = 7168
H = 64
NOPE = 128
ROPE = 64
LATENT = 512
VDIM = 128
BLOCK = 128
LEN = 4096


def rope_noise(key):
    return jax.random.truncated_normal(key, -6.0, 6.0, (LEN, ROPE), jnp.float32)


def draw_latent_keys(key, part):
    shared = rope_noise(key)
    key = jax.random.fold_in(key, 11)
    latent = jax.random.truncated_normal(key, -6.0, 6.0, (LEN, LATENT), jnp.float32)
    rotary = shared
    return jnp.concatenate([latent, rotary], axis=1).astype(jnp.bfloat16)


def draw_queries(key, part):
    key = jax.random.fold_in(key, 12)
    first_key, second_key = jax.random.split(key)
    content = 1.5 * jax.random.truncated_normal(first_key, -6.0, 6.0, (LEN, H, NOPE), jnp.float32)
    rotary = jax.random.truncated_normal(second_key, -6.0, 6.0, (LEN, H, ROPE), jnp.float32)
    joined = jnp.concatenate([content, rotary], axis=2)
    return joined.reshape(LEN, H * (NOPE + ROPE)).astype(jnp.bfloat16)


def place_ends(values, stream_key, least, high):
    shape = values.shape
    place = [jax.random.randint(jax.random.fold_in(stream_key, axis), (), 0, shape[axis]) for axis in range(len(shape))]
    values = values.at[tuple(place)].set(least)
    longest = shape.index(max(shape))
    place[longest] = (place[longest] + 1) % shape[longest]
    return values.at[tuple(place)].set(high)


def level_of(rng, shape, shards, low, high):
    def one(position, parts):
        heights = jax.random.uniform(jax.random.fold_in(jax.random.fold_in(rng, 6), position), (parts,), jnp.float32, low / len(shards), high / len(shards))
        return jnp.repeat(jnp.exp(heights), shape[position] // parts).reshape((-1,) + (1,) * (len(shape) - position - 1))

    loudness = one(*shards[0])
    for cut in shards[1:]:
        loudness = loudness * one(*cut)
    return loudness


def centred(rng, extent, scale, most, pieces=(), kind=jnp.bfloat16):
    result = jax.random.normal(rng, extent, jnp.float32) * scale
    if len(pieces) > 0:
        result = level_of(rng, extent, pieces, -0.22, 0.18) * result
    return jnp.clip(result, min=-most, max=most).astype(kind)


def setup_inputs(seed: int = 0) -> dict:
    arg_keys = jax.random.split(jax.random.key(seed), 9)
    return {
        "queries": draw_queries(jax.random.fold_in(arg_keys[8], 71), 0),
        "latent_keys": draw_latent_keys(jax.random.fold_in(arg_keys[8], 71), 0),
        "up_keys": centred(arg_keys[2], (H, NOPE, LATENT), NOPE ** -0.5, 0.5, ((0, 8), (1, 16))),
        "up_values": centred(arg_keys[3], (H, LATENT, VDIM), LATENT ** -0.5, 0.25, ((0, 8), (1, 16))),
        "out_weight": centred(arg_keys[4], (H, VDIM, D), (H * 16) ** -0.5, 0.1875, ((0, 8), (2, 16))),
        "keys_scale": place_ends(jax.random.randint(arg_keys[5], (H, LATENT // BLOCK), -1, 2), jax.random.fold_in(arg_keys[5], 1), -1, 1).astype(jnp.int32),
        "values_scale": place_ends(jax.random.randint(arg_keys[6], (H, LATENT // BLOCK), -1, 2), jax.random.fold_in(arg_keys[6], 1), -1, 1).astype(jnp.int32),
        "out_scale": place_ends(jax.random.randint(arg_keys[7], (H, D // BLOCK), -1, 2), jax.random.fold_in(arg_keys[7], 1), -1, 1).astype(jnp.int32),
    }


def rounded(values):
    return lax.optimization_barrier(values.astype(jnp.bfloat16)).astype(jnp.float32)


def exponent_factor(exponents, block_size):
    return jnp.repeat(jnp.exp2(exponents.astype(jnp.float32)), block_size, axis=1)


def reference(queries, latent_keys, up_keys, up_values, out_weight, keys_scale, values_scale, out_scale):
    keys_weight = (up_keys.astype(jnp.float32) * exponent_factor(keys_scale, BLOCK)[:, None, :]).astype(jnp.bfloat16)
    values_weight = (up_values.astype(jnp.float32) * exponent_factor(values_scale, BLOCK)[:, :, None]).astype(jnp.bfloat16)
    full_out = (out_weight.astype(jnp.float32) * exponent_factor(out_scale, BLOCK)[:, None, :]).astype(jnp.bfloat16)
    grouped = queries.reshape(LEN, H, NOPE + ROPE).transpose(1, 0, 2)
    places = jnp.arange(LEN, dtype=jnp.int32)
    causal = places[:, None] >= places[None, :]
    keys_float = latent_keys.astype(jnp.float32)
    score_scale = (NOPE + ROPE) ** -0.5
    highest = lax.Precision.HIGHEST

    def one_head(inputs):
        head_queries, head_keys_weight, head_values_weight = inputs
        latent_query = rounded(jnp.dot(head_queries[:, :NOPE].astype(jnp.float32), head_keys_weight.astype(jnp.float32), precision=highest))
        joined = jnp.concatenate([latent_query, head_queries[:, NOPE:].astype(jnp.float32)], axis=1)
        scores = jnp.dot(joined, keys_float.T, precision=highest) * score_scale
        scores = jnp.where(causal, scores, -jnp.inf)
        largest = jnp.max(scores, axis=1, keepdims=True)
        weights = jnp.where(causal, jnp.exp(scores - largest), 0.0)
        totals = jnp.sum(weights, axis=1, keepdims=True)
        mixture = jnp.dot(rounded(weights), keys_float[:, :LATENT], precision=highest) / totals
        head_latent = rounded(mixture)
        return jnp.dot(head_latent, head_values_weight.astype(jnp.float32), precision=highest).astype(jnp.bfloat16)

    head_value = lax.map(one_head, (grouped, keys_weight, values_weight))
    mixed = jnp.einsum("htv,hvd->td", head_value.astype(jnp.float32), full_out.astype(jnp.float32), precision=highest)
    return mixed.astype(jnp.bfloat16)
```

```python
import functools

import jax
import jax.numpy as jnp
from jax import lax
from jax.experimental import pallas as pl
from jax.experimental.pallas import tpu as pltpu
from jax.sharding import PartitionSpec as P

NOPE = 128
ROPE = 64
HEAD = NOPE + ROPE
LATENT = 512
WIDE = LATENT + ROPE
VDIM = 128
HEADS = 8
TOKENS = 256
CHUNK = 4 * TOKENS
PAIR = 2 * TOKENS
COLS = 448
MESH = pl.DeviceIdType.MESH
FACTOR = (NOPE + ROPE) ** (-0.5) * 1.4426950408889634
F32 = jnp.float32
BF16 = jnp.bfloat16

PEERS = (
    [(0, d, 0, k) for d in (1, 2, 3) for k in (0, 1)]
    + [(d, 0, 0, k) for d in (1, 2, 3) for k in (0, 1)]
    + [(0, 0, d, 0) for d in (1, 2, 3)]
    + [(0, 0, 0, 1)]
)


def power(exponent):
    return jnp.where(exponent > 0, 2.0, jnp.where(exponent < 0, 0.5, 1.0)).astype(F32)


def lane_factor(values, width, shift):
    block = (lax.broadcasted_iota(jnp.int32, (1, width), 1) + shift) // 128
    result = jnp.full((1, width), values[0], F32)
    for k in range(1, len(values)):
        result = jnp.where(block == k, values[k], result)
    return result


def kernel(
    queries, latent_keys, up_keys, up_values, out_weight, keys_scale, values_scale, out_scale,
    out,
    kbuf, upk, upv, qbuf, acc, mx, ls, wbuf, wsend, abuf, cbuf, land1, land0, fin, outbuf,
    ssem, sw, sa, sas, sc, sl, rk1x, rk1y, rkz, rks, ru1, ru2, rv1, rv2, rwn, rwo, ra, ras, rl1, rl0, rf,
):
    ctx = lax.axis_index("ctx")
    shard = lax.axis_index("shard")
    y, x, z, c = ctx // 4, ctx % 4, shard // 2, shard % 2
    head_first = shard * HEADS

    def at(dy=0, dx=0, dz=0, dc=0):
        return (((y + dy) % 4) * 4 + (x + dx) % 4, ((z + dz) % 4) * 2 + (c + dc) % 2)

    pending = []
    counter = [0]

    def send(src, dst, recv, target):
        k = counter[0]
        counter[0] += 1
        copy = pltpu.make_async_remote_copy(
            src_ref=src, dst_ref=dst, send_sem=ssem.at[k], recv_sem=recv,
            device_id=target, device_id_type=MESH,
        )
        copy.start()
        pending.append((src, ssem.at[k]))

    def arrived(ref, sem):
        pltpu.make_async_copy(ref, ref, sem).wait()

    for half in range(2):
        rows = []
        for k in range(4):
            h = half * 4 + k
            f = lane_factor([power(keys_scale[head_first + h, b]) for b in range(4)], LATENT, 0)
            rows.append(up_keys[h].astype(F32) * f)
        upk[half, pl.ds(y, 1), pl.ds(x, 1)] = jnp.concatenate(rows, axis=0).astype(BF16)[None, None]
    for h in range(HEADS):
        f = power(values_scale[head_first + h, y])
        upv[pl.ds(y, 1), pl.ds(x, 1), h * 32 : (h + 1) * 32, :] = (
            (up_values[h].astype(F32) * f).astype(BF16)[None, None]
        )
    own_rows = pl.ds(shard * 32, 32)
    mine = pl.ds(shard * 128, 128)
    own_place = pl.ds(shard * 128 + x * 32, 32)

    barrier = pltpu.get_barrier_semaphore()
    for dy, dx, dz, dc in PEERS:
        pl.semaphore_signal(barrier, inc=1, device_id=at(dy, dx, dz, dc), device_id_type=MESH)
    pl.semaphore_wait(barrier, len(PEERS))

    for d in (1, 3, 2):
        send(latent_keys.at[own_rows], kbuf.at[y, own_place], rk1x, at(dx=d))
    pltpu.make_async_copy(latent_keys.at[own_rows], kbuf.at[y, own_place], rk1x).start()
    for d in (1, 3, 2):
        send(upk.at[:, y, x], upk.at[:, y, x], ru1.at[d], at(dy=d))

    def keys_along_z(i):
        j = (y + 4 - i) % 4
        for d in (1, 3, 2):
            send(kbuf.at[j, mine], kbuf.at[j, mine], rkz.at[i, d], at(dz=d))
        send(kbuf.at[j, mine], kbuf.at[j, mine], rks.at[i], at(dc=1))

    def keys_to_sibling(i):
        j = (y + 4 - i) % 4
        for d in (1, 3, 2):
            z_from = (z + 4 - d) % 4
            part = kbuf.at[j, pl.ds((z_from * 2 + c) * 128, 128)]
            arrived(part, rkz.at[i, d])
            send(part, part, rks.at[i], at(dc=1))

    def keys_ready(i):
        arrived(kbuf.at[(y + 4 - i) % 4, pl.ds(0, 512)], rks.at[i])

    arrived(kbuf.at[y, mine], rk1x)
    keys_along_z(0)
    for d in (1, 2, 3):
        send(kbuf.at[y, mine], kbuf.at[y, mine], rk1y.at[d], at(dy=d))
    for d in (1, 2, 3):
        arrived(upk.at[:, (y + 4 - d) % 4, x], ru1.at[d])
    for half in range(2):
        for d in (1, 3, 2):
            send(upk.at[half, :, x], upk.at[half, :, x], ru2.at[half, d], at(dx=d))
    for d in (1, 3, 2):
        send(upv.at[y, x], upv.at[y, x], rv1.at[d], at(dy=d))

    first_block = (ctx * 7) // 2
    shift = (ctx % 2) * 64
    for h in range(HEADS):
        f = lane_factor(
            [power(out_scale[head_first + h, first_block + b]) for b in range(4)], COLS, shift
        )
        wsend[h * VDIM : (h + 1) * VDIM, :] = (out_weight[h].astype(F32) * f).astype(BF16)
    owner = y // 2
    up_one, down_one = (((y + 1) % 4) * 4 + x, z * 2 + owner), (((y + 3) % 4) * 4 + x, z * 2 + owner)
    for order in range(2):
        part_up, part_down = pl.ds(order * 512, 512), pl.ds((1 - order) * 512, 512)
        send(wsend.at[part_up], wbuf.at[y % 2, c, part_up], rwn.at[c, order], up_one)
        send(wsend.at[part_down], wbuf.at[y % 2, c, part_down], rwn.at[c, 1 - order], down_one)
    own_weight = owner == c

    @pl.when(own_weight)
    def _():
        pltpu.make_async_copy(wsend, wbuf.at[y % 2, c], rwo.at[c]).start()

    sibling_weight = pltpu.make_async_remote_copy(
        src_ref=wsend, dst_ref=wbuf.at[y % 2, c], send_sem=sw.at[0], recv_sem=rwo.at[c],
        device_id=at(dc=1), device_id_type=MESH,
    )

    @pl.when(jnp.logical_not(own_weight))
    def _():
        sibling_weight.start()

    near_slot = (y + 1) % 2
    from_below = (2 * c + near_slot + 4 - y) % 4 == 3

    def weight_relay():
        half = jnp.where(from_below, 0, 1)
        for k in range(2):
            arrived(wbuf.at[near_slot, k, pl.ds(0, 512)], rwn.at[k, half])
        part = wbuf.at[near_slot, :, pl.ds(half * 512, 512)]
        step = jnp.where(from_below, 1, 3)
        send(part, part, rwo.at[half], (((y + step) % 4) * 4 + x, shard))

    def weight_ready():
        rest = jnp.where(from_below, 1, 0)
        for k in range(2):
            arrived(wbuf.at[near_slot, k, pl.ds(0, 512)], rwn.at[k, rest])
        for k in range(2):
            arrived(wbuf.at[y % 2, k], rwo.at[k])

    def make_queries(half):
        for d in (1, 2, 3):
            arrived(upk.at[half, :, (x + 4 - d) % 4], ru2.at[half, d])
        tiles = upk[half].astype(F32).reshape(16, 4, 8, LATENT)
        for k in range(4):
            h = half * 4 + k
            weight = tiles[:, k].reshape(NOPE, LATENT).astype(BF16)
            content = queries[:, h * HEAD : h * HEAD + NOPE]
            latent = jnp.dot(content, weight, preferred_element_type=F32).astype(BF16)
            qbuf[h * TOKENS : (h + 1) * TOKENS, :LATENT] = latent
            qbuf[h * TOKENS : (h + 1) * TOKENS, LATENT:] = queries[:, h * HEAD + NOPE : (h + 1) * HEAD]

    def update(pair, i):
        rows = pl.ds(pair * PAIR, PAIR)
        j = (y + 4 - i) % 4
        scores = lax.dot_general(
            qbuf[rows, :], kbuf[j], (((1,), (1,)), ((), ())), preferred_element_type=F32
        )
        latent = kbuf[j, :, :LATENT]
        if i == 0:
            row = lax.broadcasted_iota(jnp.int32, (PAIR, CHUNK), 0) % TOKENS + x * TOKENS
            col = lax.broadcasted_iota(jnp.int32, (PAIR, CHUNK), 1)
            place = ((col % 128) // 32) * TOKENS + (col // 128) * 32 + col % 32
            scores = jnp.where(place <= row, scores, -1e30)
            newest = jnp.max(scores, axis=1, keepdims=True)
            weights = jnp.exp2((scores - newest) * FACTOR)
            ls[rows, :] = jnp.broadcast_to(jnp.sum(weights, axis=1, keepdims=True), (PAIR, 128))
            acc[rows, :] = jnp.dot(weights.astype(BF16), latent, preferred_element_type=F32)
        else:
            last = mx[rows, :1]
            newest = jnp.maximum(last, jnp.max(scores, axis=1, keepdims=True))
            weights = jnp.exp2((scores - newest) * FACTOR)
            decay = jnp.exp2((last - newest) * FACTOR)
            ls[rows, :] = ls[rows, :] * decay + jnp.sum(weights, axis=1, keepdims=True)
            acc[rows, :] = acc[rows, :] * decay + jnp.dot(
                weights.astype(BF16), latent, preferred_element_type=F32
            )
        mx[rows, :] = jnp.broadcast_to(newest, (PAIR, 128))

    def pair_lanes(pair, core):
        return pl.ds(pl.multiple_of(core * 1024 + pair * 256, 256), 256)

    def finish(pair):
        for k in range(2):
            h = pair * 2 + k
            rows = pl.ds(h * TOKENS, TOKENS)
            head_latent = (acc[rows, :] / ls[rows, :1]).astype(BF16)
            tile = upv[:, :, h * 32 : (h + 1) * 32, :].reshape(LATENT, VDIM)
            value = jnp.dot(head_latent, tile, preferred_element_type=F32).astype(BF16)
            lanes = pl.ds(pl.multiple_of(c * 1024 + h * VDIM, VDIM), VDIM)
            abuf[pl.ds(x, 1), :, lanes] = value[None]
        part = abuf.at[x, :, pair_lanes(pair, c)]
        for d in (1, 3, 2):
            send(part, part, ra.at[pair, d], at(dx=d))

    def values_to_sibling(pair):
        for d in (1, 2, 3):
            arrived(abuf.at[(x + 4 - d) % 4, :, pair_lanes(pair, c)], ra.at[pair, d])
        part = abuf.at[:, :, pair_lanes(pair, c)]
        send(part, part, ras.at[pair], at(dc=1))

    def values_ready(pair):
        arrived(abuf.at[:, :, pair_lanes(pair, 1 - c)], ras.at[pair])

    make_queries(0)
    keys_to_sibling(0)
    for d in (1, 2, 3):
        arrived(upv.at[(y + 4 - d) % 4, x], rv1.at[d])
    for d in (1, 3, 2):
        send(upv.at[:, x], upv.at[:, x], rv2.at[d], at(dx=d))
    keys_ready(0)
    for i in range(4):
        if i < 3:
            arrived(kbuf.at[(y + 3 - i) % 4, mine], rk1y.at[i + 1])
            keys_along_z(i + 1)
        if i == 2:
            weight_relay()
        for pair in range(2):
            if i == 0:
                update(pair, i)
            else:
                pl.when(y >= i)(functools.partial(update, pair, i))
            if pair == 0 and i < 3:
                keys_to_sibling(i + 1)
        if i < 3:
            keys_ready(i + 1)
    make_queries(1)
    for d in (1, 2, 3):
        arrived(upv.at[:, (x + 4 - d) % 4], rv2.at[d])
    finish(0)
    finish(1)
    for pair in range(2, 4):
        for i in range(4):
            if i == 0:
                update(pair, i)
            else:
                pl.when(y >= i)(functools.partial(update, pair, i))
        values_to_sibling(pair - 2)
        finish(pair)
    values_to_sibling(2)
    values_to_sibling(3)
    weight_ready()
    for pair in range(4):
        values_ready(pair)

    near = (z + 1) % 2
    other = z % 2
    is_own = z // 2 == c
    near_up = (2 * c + near + 4 - z) % 4 == 1
    near_half = jnp.where(near_up, 0, 1)
    z_near = jnp.where(near_up, 1, 3)

    def project(slot, t):
        part = jnp.dot(abuf[t, :, :1024], wbuf[slot, 0], preferred_element_type=F32)
        part += jnp.dot(abuf[t, :, 1024:], wbuf[slot, 1], preferred_element_type=F32)
        cbuf[slot, t] = part.astype(BF16)

    def far_copy(t, half):
        return pltpu.make_async_remote_copy(
            src_ref=cbuf.at[other, t, pl.ds(half * 128, 128)], dst_ref=land1.at[t],
            send_sem=sc.at[t, half], recv_sem=rl1.at[t],
            device_id=at(dz=1 if half == 0 else 3), device_id_type=MESH,
        )

    def near_copy(t):
        return pltpu.make_async_remote_copy(
            src_ref=cbuf.at[near, t], dst_ref=land0.at[near_half, t],
            send_sem=sl.at[t], recv_sem=rl0.at[near_half, t],
            device_id=at(dz=z_near), device_id_type=MESH,
        )

    first = jnp.where(is_own, near, other)

    def first_step(t, carry):
        project(first, t)

        @pl.when(jnp.logical_not(is_own))
        def _():
            far_copy(t, 0).start()
            far_copy(t, 1).start()

        return carry

    def second_step(t, carry):
        project(1 - first, t)
        return carry

    def near_step(t, carry):
        arrived(land1.at[t], rl1.at[t])
        rows = pl.ds(near_half * 128, 128)
        total = cbuf[near, t, rows].astype(F32) + land1[t].astype(F32)
        cbuf[near, t, rows] = total.astype(BF16)
        near_copy(t).start()
        return carry

    lax.fori_loop(0, 4, first_step, 0)
    lax.fori_loop(0, 4, second_step, 0)
    lax.fori_loop(0, 4, near_step, 0)

    receiver = x // 2

    def final_copy(t):
        return pltpu.make_async_remote_copy(
            src_ref=fin.at[t], dst_ref=outbuf.at[x % 2], send_sem=sa.at[t], recv_sem=rf.at[x % 2],
            device_id=(y * 4 + t, z * 2 + receiver), device_id_type=MESH,
        )

    def local_copy(t):
        return pltpu.make_async_copy(fin.at[t], outbuf.at[x % 2], rf.at[x % 2])

    def final_step(t, carry):
        arrived(land0.at[0, t], rl0.at[0, t])
        arrived(land0.at[1, t], rl0.at[1, t])
        total = cbuf[other, t].astype(F32) + land0[0, t].astype(F32) + land0[1, t].astype(F32)
        fin[t] = total.astype(BF16)
        here = jnp.logical_and(t == x, receiver == c)

        @pl.when(here)
        def _():
            local_copy(t).start()

        @pl.when(jnp.logical_not(here))
        def _():
            final_copy(t).start()

        return carry

    @pl.when(is_own)
    def _():
        lax.fori_loop(0, 4, final_step, 0)

    for k in range(2):
        arrived(outbuf.at[k], rf.at[k])
    out[:, :COLS] = outbuf[0]
    out[:, COLS:] = outbuf[1]

    for ref, sem in pending:
        arrived(ref, sem)

    @pl.when(jnp.logical_not(own_weight))
    def _():
        sibling_weight.wait_send()

    def sent_near(t, carry):
        near_copy(t).wait_send()
        return carry

    def sent_far(t, carry):
        far_copy(t, 0).wait_send()
        far_copy(t, 1).wait_send()
        return carry

    def sent_final(t, carry):
        @pl.when(jnp.logical_not(jnp.logical_and(t == x, receiver == c)))
        def _():
            final_copy(t).wait_send()

        return carry

    lax.fori_loop(0, 4, sent_near, 0)

    @pl.when(jnp.logical_not(is_own))
    def _():
        lax.fori_loop(0, 4, sent_far, 0)

    @pl.when(is_own)
    def _():
        lax.fori_loop(0, 4, sent_final, 0)


def body(queries, latent_keys, up_keys, up_values, out_weight, keys_scale, values_scale, out_scale):
    vmem = pl.BlockSpec(memory_space=pltpu.VMEM)
    smem = pl.BlockSpec(memory_space=pltpu.SMEM)
    dma = pltpu.SemaphoreType.DMA
    return pl.pallas_call(
        kernel,
        out_shape=jax.ShapeDtypeStruct((TOKENS, 2 * COLS), BF16),
        in_specs=[vmem] * 5 + [smem] * 3,
        out_specs=vmem,
        scratch_shapes=[
            pltpu.VMEM((4, CHUNK, WIDE), BF16),
            pltpu.VMEM((2, 4, 4, 32, LATENT), BF16),
            pltpu.VMEM((4, 4, 256, VDIM), BF16),
            pltpu.VMEM((HEADS * TOKENS, WIDE), BF16),
            pltpu.VMEM((HEADS * TOKENS, LATENT), F32),
            pltpu.VMEM((HEADS * TOKENS, 128), F32),
            pltpu.VMEM((HEADS * TOKENS, 128), F32),
            pltpu.VMEM((2, 2, 1024, COLS), BF16),
            pltpu.VMEM((1024, COLS), BF16),
            pltpu.VMEM((4, TOKENS, 2048), BF16),
            pltpu.VMEM((2, 4, TOKENS, COLS), BF16),
            pltpu.VMEM((4, 128, COLS), BF16),
            pltpu.VMEM((2, 4, TOKENS, COLS), BF16),
            pltpu.VMEM((4, TOKENS, COLS), BF16),
            pltpu.VMEM((2, TOKENS, COLS), BF16),
            dma((96,)),
            dma((1,)),
            dma((4,)),
            dma((4,)),
            dma((4, 2)),
            dma((4,)),
            dma,
            dma((4,)),
            dma((4, 4)),
            dma((4,)),
            dma((4,)),
            dma((2, 4)),
            dma((4,)),
            dma((4,)),
            dma((2, 2)),
            dma((2,)),
            dma((4, 4)),
            dma((4,)),
            dma((4,)),
            dma((2, 4)),
            dma((2,)),
        ],
        compiler_params=pltpu.CompilerParams(
            collective_id=0, has_side_effects=True, vmem_limit_bytes=56 * 2**20
        ),
        name="attention",
    )(queries, latent_keys, up_keys, up_values, out_weight, keys_scale, values_scale, out_scale)


def solution(mesh):
    return jax.shard_map(
        body,
        mesh=mesh,
        in_specs=(
            P("ctx", "shard"),
            P("ctx", None),
            P("shard", "ctx", None),
            P("shard", "ctx", None),
            P("shard", None, "ctx"),
            P(),
            P(),
            P(),
        ),
        out_specs=P("ctx", "shard"),
        check_vma=False,
    )
```

```python
import functools

import jax
import jax.numpy as jnp
from jax import lax
from jax.experimental import pallas as pl
from jax.experimental.pallas import tpu as pltpu
from jax.sharding import PartitionSpec as P

NOPE = 128
ROPE = 64
HEAD = NOPE + ROPE
LATENT = 512
WIDE = LATENT + ROPE
VDIM = 128
HEADS = 8
TOKENS = 256
CHUNK = 4 * TOKENS
COLS = 448
PIECE = WIDE // 4
MESH = pl.DeviceIdType.MESH
FACTOR = (NOPE + ROPE) ** (-0.5) * 1.4426950408889634
F32 = jnp.float32
BF16 = jnp.bfloat16

PEERS = (
    [(0, d, 0, k) for d in (1, 2, 3) for k in (0, 1)]
    + [(d, 0, 0, k) for d in (1, 2, 3) for k in (0, 1)]
    + [(0, 0, d, 0) for d in (1, 2, 3)]
    + [(0, 0, 0, 1)]
)


def power(exponent):
    return jnp.where(exponent > 0, 2.0, jnp.where(exponent < 0, 0.5, 1.0)).astype(F32)


def block_factor(values, shape, dim, shift):
    block = (lax.broadcasted_iota(jnp.int32, shape, dim) + shift) // 128
    result = jnp.full(shape, values[0], F32)
    for k in range(1, len(values)):
        result = jnp.where(block == k, values[k], result)
    return result


def kernel(
    queries, latent_keys, up_keys, up_values, out_weight, keys_scale, values_scale, out_scale,
    out,
    kbuf, upk, upv, qbuf, acc, mx, ls, wbuf, wsend, abuf, cbuf, land1, land0, fin, outbuf,
    ssem, sw, sa, sc, sl, rk1x, rk1y, rkz, rks, ru1, ru2, rv1, rv2, rwn, rwo, ra, ras, rl1, rl0, rf,
):
    ctx = lax.axis_index("ctx")
    shard = lax.axis_index("shard")
    y, x, z, c = ctx // 4, ctx % 4, shard // 2, shard % 2
    head_first = shard * HEADS

    def at(dy=0, dx=0, dz=0, dc=0):
        return (((y + dy) % 4) * 4 + (x + dx) % 4, ((z + dz) % 4) * 2 + (c + dc) % 2)

    barrier = pltpu.get_barrier_semaphore()
    for dy, dx, dz, dc in PEERS:
        pl.semaphore_signal(barrier, inc=1, device_id=at(dy, dx, dz, dc), device_id_type=MESH)

    pending = []
    counter = [0]

    def send(src, dst, recv, target, condition=None):
        k = counter[0]
        counter[0] += 1
        copy = pltpu.make_async_remote_copy(
            src_ref=src, dst_ref=dst, send_sem=ssem.at[k], recv_sem=recv,
            device_id=target, device_id_type=MESH,
        )
        copy.start()
        pending.append((src, k, condition))

    def arrived(ref, sem):
        pltpu.make_async_copy(ref, ref, sem).wait()

    for half in range(2):
        rows = []
        for k in range(4):
            h = half * 4 + k
            f = block_factor(
                [power(keys_scale[b, head_first + h]) for b in range(4)], (1, LATENT), 1, 0
            )
            rows.append(up_keys[h].astype(F32) * f)
        upk[half, pl.ds(y, 1), pl.ds(x, 1)] = jnp.concatenate(rows, axis=0).astype(BF16)[None, None]

    for h in range(HEADS):
        f = power(values_scale[y, head_first + h])
        upv[pl.ds(y, 1), pl.ds(x, 1), h * 32 : (h + 1) * 32, :] = (
            (up_values[h].astype(F32) * f).astype(BF16)[None, None]
        )

    chunk = [(y + 4 - i) % 4 for i in range(4)]
    features = [pl.ds(((z + d) % 4) * PIECE, PIECE) for d in range(4)]
    my_lanes = pl.ds(pl.multiple_of(c * 512, 512), 512)
    my_halves = [pl.ds(pl.multiple_of(c * 512 + k * 256, 256), 256) for k in range(2)]
    its_lanes = pl.ds(pl.multiple_of((1 - c) * 512, 512), 512)
    own_lanes = pl.ds(pl.multiple_of(c * 128, 128), 128)
    own_place = pl.ds(pl.multiple_of(c * 512 + x * 128, 128), 128)

    pl.semaphore_wait(barrier, len(PEERS))

    own_keys, own_slot = latent_keys.at[features[0], own_lanes], kbuf.at[y, features[0], own_place]
    for d in (1, 3, 2):
        send(own_keys, own_slot, rk1x, at(dx=d))
    pltpu.make_async_copy(own_keys, own_slot, rk1x).start()
    for d in (1, 3, 2):
        piece = upk.at[0, y, x]
        send(piece, piece, ru1.at[0, d], at(dy=d))

    def needed(i, action):
        if i == 0:
            action()
        else:
            pl.when(y >= i)(action)

    def keys_along_z(i):
        part = kbuf.at[chunk[i], features[0], my_lanes]
        condition = None if i == 0 else y >= i

        def action():
            if i > 0:
                arrived(part, rk1y.at[i])
            for d in (1, 3):
                send(part, part, rkz.at[i, d], at(dz=d), condition)
            send(part, part, rks.at[i], at(dc=1), condition)

        needed(i, action)

    def keys_relay(i):
        condition = None if i == 0 else y >= i

        def action():
            for d in (1, 3):
                part = kbuf.at[chunk[i], features[4 - d], my_lanes]
                arrived(part, rkz.at[i, d])
                half = kbuf.at[chunk[i], features[4 - d], my_halves[d // 2]]
                send(half, half, rkz.at[i, 2], at(dz=d), condition)
                send(part, part, rks.at[i], at(dc=1), condition)

        needed(i, action)

    def keys_far(i):
        condition = None if i == 0 else y >= i

        def action():
            part = kbuf.at[chunk[i], features[2], my_lanes]
            arrived(part, rkz.at[i, 2])
            send(part, part, rks.at[i], at(dc=1), condition)

        needed(i, action)

    def keys_ready(i):
        needed(i, lambda: arrived(kbuf.at[chunk[i], :, its_lanes], rks.at[i]))

    first_block = (ctx * 7) // 2
    shift = (ctx % 2) * 64
    for h in range(HEADS):
        f = block_factor(
            [power(out_scale[first_block + b, head_first + h]) for b in range(4)], (COLS, 1), 0, shift
        )
        wsend[:, h * VDIM : (h + 1) * VDIM] = (out_weight[h].astype(F32) * f).astype(BF16)

    arrived(kbuf.at[y, features[0], my_lanes], rk1x)
    keys_along_z(0)
    for d in (1, 2, 3):
        part = kbuf.at[y, features[0], my_lanes]
        condition = y + d < 4
        pl.when(condition)(lambda: send(part, part, rk1y.at[d], at(dy=d), condition))
    y_from = [(y + 4 - d) % 4 for d in range(4)]
    x_from = [(x + 4 - d) % 4 for d in range(4)]
    for d in (1, 3, 2):
        arrived(upk.at[0, y_from[d], x], ru1.at[0, d])
    for d in (1, 3, 2):
        send(upk.at[0, :, x], upk.at[0, :, x], ru2.at[0, d], at(dx=d))
    for d in (1, 3, 2):
        send(upk.at[1, y, x], upk.at[1, y, x], ru1.at[1, d], at(dy=d))
    for d in (1, 3, 2):
        send(upv.at[y, x], upv.at[y, x], rv1.at[d], at(dy=d))
    keys_relay(0)
    keys_along_z(1)
    for d in (1, 3, 2):
        arrived(upk.at[0, :, x_from[d]], ru2.at[0, d])

    owner = y // 2
    up_one, down_one = (((y + 1) % 4) * 4 + x, z * 2 + owner), (((y + 3) % 4) * 4 + x, z * 2 + owner)
    weight_lanes = pl.ds(pl.multiple_of(c * 1024, 1024), 1024)
    weight_rows = [pl.ds(0, COLS // 2), pl.ds(COLS // 2, COLS // 2)]
    for order in range(2):
        for half, target in ((order, up_one), (1 - order, down_one)):
            rows = weight_rows[half]
            send(wsend.at[rows], wbuf.at[y % 2, rows, weight_lanes], rwn.at[c, half], target)
    own_weight = owner == c

    @pl.when(own_weight)
    def _():
        pltpu.make_async_copy(wsend, wbuf.at[y % 2, :, weight_lanes], rwo.at[c]).start()

    sibling_weight = pltpu.make_async_remote_copy(
        src_ref=wsend, dst_ref=wbuf.at[y % 2, :, weight_lanes], send_sem=sw.at[0], recv_sem=rwo.at[c],
        device_id=at(dc=1), device_id_type=MESH,
    )

    @pl.when(jnp.logical_not(own_weight))
    def _():
        sibling_weight.start()

    near_slot = (y + 1) % 2
    from_below = (2 * c + near_slot + 4 - y) % 4 == 3

    def weight_relay():
        half = jnp.where(from_below, 0, 1)
        for k in range(2):
            arrived(wbuf.at[near_slot, weight_rows[0], pl.ds(0, 1024)], rwn.at[k, half])
        part = wbuf.at[near_slot, pl.ds(half * (COLS // 2), COLS // 2)]
        step = jnp.where(from_below, 1, 3)
        send(part, part, rwo.at[half], (((y + step) % 4) * 4 + x, shard))

    def weight_ready():
        rest = jnp.where(from_below, 1, 0)
        for k in range(2):
            arrived(wbuf.at[near_slot, weight_rows[0], pl.ds(0, 1024)], rwn.at[k, rest])
        for k in range(2):
            arrived(wbuf.at[y % 2, :, pl.ds(0, 1024)], rwo.at[k])

    def make_queries(half):
        tiles = upk[half].astype(F32).reshape(16, 4, 8, LATENT)
        for k in range(4):
            h = half * 4 + k
            weight = tiles[:, k].reshape(NOPE, LATENT).astype(BF16)
            content = queries[:, h * HEAD : h * HEAD + NOPE]
            latent = jnp.dot(content, weight, preferred_element_type=F32).astype(BF16)
            rotary = queries[:, h * HEAD + NOPE : (h + 1) * HEAD]
            for part in range(2):
                rows = slice(part * 1024 + h * 128, part * 1024 + (h + 1) * 128)
                tokens = slice(part * 128, (part + 1) * 128)
                qbuf[rows, :LATENT] = latent[tokens]
                qbuf[rows, LATENT:] = rotary[tokens]

    def chunk_of(i):
        return (y + 4 - i) % 4

    def attend(units, first=False):

        def score(i, part, group):
            first_row = part * 1024 + group * 512
            scores = jnp.dot(
                qbuf[first_row : first_row + 512, :], kbuf[chunk_of(i)], preferred_element_type=F32
            )
            if first:
                row = lax.broadcasted_iota(jnp.int32, (512, CHUNK), 0) % 128 + (x * TOKENS + part * 128)
                col = lax.broadcasted_iota(jnp.int32, (512, CHUNK), 1)
                place = ((col % 512) // 128) * TOKENS + (col // 512) * 128 + col % 128
                scores = jnp.where(place <= row, scores, -1e30)
            return scores

        def mix(scores, i, part, group):
            rows = slice(part * 1024 + group * 512, part * 1024 + group * 512 + 512)
            newest = jnp.max(scores, axis=1, keepdims=True)
            if not first:
                last = mx[rows, :1]
                newest = jnp.maximum(last, newest)
            weights = jnp.exp2((scores - newest) * FACTOR)
            total = jnp.sum(weights, axis=1, keepdims=True)
            mx[rows, :] = jnp.broadcast_to(newest, (512, 128))
            mixture = lax.dot_general(
                weights.astype(BF16), kbuf[chunk_of(i), :LATENT], (((1,), (1,)), ((), ())),
                preferred_element_type=F32,
            )
            if first:
                ls[rows, :] = jnp.broadcast_to(total, (512, 128))
                acc[rows, :] = mixture
            else:
                decay = jnp.exp2((last - newest) * FACTOR)
                ls[rows, :] = ls[rows, :] * decay + total
                acc[rows, :] = acc[rows, :] * decay + mixture

        scores = score(*units[0])
        for n, unit in enumerate(units):
            following = score(*units[n + 1]) if n + 1 < len(units) else None
            mix(scores, *unit)
            scores = following

    def value_lanes(core):
        return pl.ds(pl.multiple_of(core * 1024, 1024), 1024)

    def value_place(part, place, core):
        rows = pl.ds(pl.multiple_of((place % 2) * 128, 128), 128)
        return abuf.at[part * 2 + place // 2, rows, value_lanes(core)]

    def finish(part, group):
        for h in range(group * 4, group * 4 + 4):
            rows = slice(part * 1024 + h * 128, part * 1024 + (h + 1) * 128)
            head_latent = (acc[rows, :] / ls[rows, :1]).astype(BF16)
            tile = upv[:, :, h * 32 : (h + 1) * 32, :].reshape(LATENT, VDIM)
            value = jnp.dot(head_latent, tile, preferred_element_type=F32).astype(BF16)
            lanes = pl.ds(pl.multiple_of(c * 1024 + h * VDIM, VDIM), VDIM)
            abuf[part * 2 + x // 2, pl.ds(pl.multiple_of((x % 2) * 128, 128), 128), lanes] = value
        rows = pl.ds(pl.multiple_of((x % 2) * 128, 128), 128)
        lanes = pl.ds(pl.multiple_of(c * 1024 + group * 512, 512), 512)
        piece = abuf.at[part * 2 + x // 2, rows, lanes]
        for d in (1, 3, 2):
            send(piece, piece, ra.at[part, d], at(dx=d))
        send(piece, piece, ras.at[part], at(dc=1))

    def values_forward(part):
        for d in (1, 3, 2):
            piece = value_place(part, x_from[d], c)
            arrived(piece, ra.at[part, d])
            send(piece, piece, ras.at[part], at(dc=1))

    def values_ready(part):
        arrived(abuf.at[pl.ds(part * 2, 2), :, value_lanes(1 - c)], ras.at[part])

    def rest_of_chunks(part, group):
        @pl.when(y == 3)
        def _():
            attend([(i, part, group) for i in (1, 2, 3)])

        @pl.when(y < 3)
        def _():
            def step(i, carry):
                attend([(i, part, group)])
                return carry

            lax.fori_loop(1, y + 1, step, 0)

    for d in (1, 3, 2):
        arrived(upk.at[1, y_from[d], x], ru1.at[1, d])
    for d in (1, 3, 2):
        send(upk.at[1, :, x], upk.at[1, :, x], ru2.at[1, d], at(dx=d))
    make_queries(0)
    keys_far(0)
    keys_along_z(2)
    keys_ready(0)
    attend([(0, 0, 0), (0, 1, 0)], True)
    keys_relay(1)
    keys_along_z(3)
    for d in (1, 3, 2):
        arrived(upk.at[1, :, x_from[d]], ru2.at[1, d])
    for d in (1, 3, 2):
        arrived(upv.at[y_from[d], x], rv1.at[d])
    for d in (1, 3, 2):
        send(upv.at[:, x], upv.at[:, x], rv2.at[d], at(dx=d))
    make_queries(1)
    attend([(0, 0, 1), (0, 1, 1)], True)
    keys_far(1)
    keys_relay(2)
    keys_ready(1)
    needed(1, lambda: attend([(1, 0, 0), (1, 0, 1)]))
    keys_far(2)
    keys_relay(3)
    keys_ready(2)
    needed(2, lambda: attend([(2, 0, 0), (2, 0, 1)]))
    weight_relay()
    keys_far(3)
    for d in (1, 3, 2):
        arrived(upv.at[:, x_from[d]], rv2.at[d])
    keys_ready(3)
    needed(3, lambda: attend([(3, 0, 0), (3, 0, 1)]))
    finish(0, 0)
    finish(0, 1)
    rest_of_chunks(1, 0)
    finish(1, 0)
    rest_of_chunks(1, 1)
    finish(1, 1)
    values_forward(0)
    weight_ready()
    values_ready(0)

    near = (z + 1) % 2
    other = z % 2
    is_own = z // 2 == c
    near_up = (2 * c + near + 4 - z) % 4 == 1
    near_half = jnp.where(near_up, 0, 1)
    z_near = jnp.where(near_up, 1, 3)

    def project(slot, t):
        part = lax.dot_general(
            wbuf[slot], abuf[t], (((1,), (1,)), ((), ())), preferred_element_type=F32
        )
        cbuf[slot, t] = part.astype(BF16)

    def far_copy(t, half):
        return pltpu.make_async_remote_copy(
            src_ref=cbuf.at[other, t, pl.ds(half * (COLS // 2), COLS // 2)], dst_ref=land1.at[t],
            send_sem=sc.at[t, half], recv_sem=rl1.at[t],
            device_id=at(dz=1 if half == 0 else 3), device_id_type=MESH,
        )

    def near_copy(t):
        return pltpu.make_async_remote_copy(
            src_ref=cbuf.at[near, t], dst_ref=land0.at[near_half, t],
            send_sem=sl.at[t], recv_sem=rl0.at[near_half, t],
            device_id=at(dz=z_near), device_id_type=MESH,
        )

    first = jnp.where(is_own, near, other)

    def first_step(t, carry):
        project(first, t)

        @pl.when(jnp.logical_not(is_own))
        def _():
            far_copy(t, 0).start()
            far_copy(t, 1).start()

        return carry

    def second_step(t, carry):
        project(1 - first, t)
        return carry

    def near_step(t, carry):
        arrived(land1.at[t], rl1.at[t])
        rows = pl.ds(near_half * (COLS // 2), COLS // 2)
        total = cbuf[near, t, rows].astype(F32) + land1[t].astype(F32)
        cbuf[near, t, rows] = total.astype(BF16)
        near_copy(t).start()
        return carry

    receiver = x // 2

    def final_copy(t, k):
        place = (t % 2) * 2 + k
        lanes = pl.ds(pl.multiple_of((t // 2) * 128, 128), 128)
        source, target = fin.at[t, :, k * 128 : (k + 1) * 128], outbuf.at[x % 2, :, lanes]
        here = jnp.logical_and(place == x, receiver == c)
        local = pltpu.make_async_copy(source, target, rf.at[x % 2])
        remote = pltpu.make_async_remote_copy(
            src_ref=source, dst_ref=target, send_sem=sa.at[t, k], recv_sem=rf.at[x % 2],
            device_id=(y * 4 + place, z * 2 + receiver), device_id_type=MESH,
        )
        return here, local, remote

    def final_step(t, carry):
        arrived(land0.at[0, t], rl0.at[0, t])
        arrived(land0.at[1, t], rl0.at[1, t])
        total = cbuf[other, t].astype(F32) + land0[0, t].astype(F32) + land0[1, t].astype(F32)
        fin[t] = total.astype(BF16)
        for k in range(2):
            here, local, remote = final_copy(t, k)
            pl.when(here)(local.start)
            pl.when(jnp.logical_not(here))(remote.start)
        return carry

    lax.fori_loop(0, 2, first_step, 0)
    lax.fori_loop(0, 2, second_step, 0)
    lax.fori_loop(0, 2, near_step, 0)
    values_forward(1)
    values_ready(1)
    lax.fori_loop(2, 4, first_step, 0)
    lax.fori_loop(2, 4, second_step, 0)

    @pl.when(is_own)
    def _():
        lax.fori_loop(0, 2, final_step, 0)

    lax.fori_loop(2, 4, near_step, 0)

    @pl.when(is_own)
    def _():
        lax.fori_loop(2, 4, final_step, 0)

    for k in range(2):
        arrived(outbuf.at[k], rf.at[k])
    out[:COLS, :] = outbuf[0]
    out[COLS:, :] = outbuf[1]

    for ref, k, condition in pending:
        if condition is None:
            arrived(ref, ssem.at[k])
        else:
            pl.when(condition)(functools.partial(lambda r, n: arrived(r, ssem.at[n]), ref, k))

    @pl.when(jnp.logical_not(own_weight))
    def _():
        sibling_weight.wait_send()

    def sent_near(t, carry):
        near_copy(t).wait_send()
        return carry

    def sent_far(t, carry):
        far_copy(t, 0).wait_send()
        far_copy(t, 1).wait_send()
        return carry

    def sent_final(t, carry):
        for k in range(2):
            here, local, remote = final_copy(t, k)
            pl.when(jnp.logical_not(here))(remote.wait_send)
        return carry

    lax.fori_loop(0, 4, sent_near, 0)

    @pl.when(jnp.logical_not(is_own))
    def _():
        lax.fori_loop(0, 4, sent_far, 0)

    @pl.when(is_own)
    def _():
        lax.fori_loop(0, 4, sent_final, 0)


def body(queries, latent_keys, up_keys, up_values, out_weight, keys_scale, values_scale, out_scale):
    vmem = pl.BlockSpec(memory_space=pltpu.VMEM)
    smem = pl.BlockSpec(memory_space=pltpu.SMEM)
    dma = pltpu.SemaphoreType.DMA
    result = pl.pallas_call(
        kernel,
        out_shape=jax.ShapeDtypeStruct((2 * COLS, TOKENS), BF16),
        in_specs=[vmem] * 5 + [smem] * 3,
        out_specs=vmem,
        scratch_shapes=[
            pltpu.VMEM((4, WIDE, CHUNK), BF16),
            pltpu.VMEM((2, 4, 4, 32, LATENT), BF16),
            pltpu.VMEM((4, 4, 256, VDIM), BF16),
            pltpu.VMEM((HEADS * TOKENS, WIDE), BF16),
            pltpu.VMEM((HEADS * TOKENS, LATENT), F32),
            pltpu.VMEM((HEADS * TOKENS, 128), F32),
            pltpu.VMEM((HEADS * TOKENS, 128), F32),
            pltpu.VMEM((2, COLS, 2048), BF16),
            pltpu.VMEM((COLS, 1024), BF16),
            pltpu.VMEM((4, TOKENS, 2048), BF16),
            pltpu.VMEM((2, 4, COLS, TOKENS), BF16),
            pltpu.VMEM((4, COLS // 2, TOKENS), BF16),
            pltpu.VMEM((2, 4, COLS, TOKENS), BF16),
            pltpu.VMEM((4, COLS, TOKENS), BF16),
            pltpu.VMEM((2, COLS, TOKENS), BF16),
            dma((128,)),
            dma((1,)),
            dma((4, 2)),
            dma((4, 2)),
            dma((4,)),
            dma,
            dma((4,)),
            dma((4, 4)),
            dma((4,)),
            dma((3, 4)),
            dma((3, 4)),
            dma((4,)),
            dma((4,)),
            dma((2, 2)),
            dma((2,)),
            dma((2, 4)),
            dma((2,)),
            dma((4,)),
            dma((2, 4)),
            dma((2,)),
        ],
        compiler_params=pltpu.CompilerParams(
            collective_id=0, has_side_effects=True, vmem_limit_bytes=56 * 2**20
        ),
        name="attention",
    )(
        queries, latent_keys.T, up_keys, up_values, out_weight.swapaxes(1, 2),
        keys_scale.T, values_scale.T, out_scale.T,
    )
    return result.T


def solution(mesh):
    return jax.shard_map(
        body,
        mesh=mesh,
        in_specs=(
            P("ctx", "shard"),
            P("ctx", None),
            P("shard", "ctx", None),
            P("shard", "ctx", None),
            P("shard", None, "ctx"),
            P(),
            P(),
            P(),
        ),
        out_specs=P("ctx", "shard"),
        check_vma=False,
    )
```

```python
import functools

import jax
import jax.numpy as jnp
from jax import lax
from jax.experimental import pallas as pl
from jax.experimental.pallas import tpu as pltpu
from jax.sharding import PartitionSpec as P

NOPE = 128
ROPE = 64
HEAD = NOPE + ROPE
LATENT = 512
WIDE = LATENT + ROPE
VDIM = 128
HEADS = 8
TOKENS = 256
CHUNK = 4 * TOKENS
COLS = 448
PIECE = WIDE // 4
MESH = pl.DeviceIdType.MESH
FACTOR = (NOPE + ROPE) ** (-0.5) * 1.4426950408889634
F32 = jnp.float32
BF16 = jnp.bfloat16

PEERS = (
    [(0, d, 0, k) for d in (1, 2, 3) for k in (0, 1)]
    + [(d, 0, 0, k) for d in (1, 2, 3) for k in (0, 1)]
    + [(0, 0, d, 0) for d in (1, 2, 3)]
    + [(0, 0, 0, 1)]
)


def power(exponent):
    return jnp.where(exponent > 0, 2.0, jnp.where(exponent < 0, 0.5, 1.0)).astype(F32)


def block_factor(values, shape, dim, shift):
    block = (lax.broadcasted_iota(jnp.int32, shape, dim) + shift) // 128
    result = jnp.full(shape, values[0], F32)
    for k in range(1, len(values)):
        result = jnp.where(block == k, values[k], result)
    return result


def kernel(
    queries, latent_keys, up_keys, up_values, out_weight, keys_scale, values_scale, out_scale,
    out,
    kbuf, upk, upv, qbuf, acc, mx, ls, wbuf, wsend, abuf, cbuf, land1, land0, fin, outbuf,
    ssem, sw, sa, sc, sl, rk1x, rk1y, rkz, rks, ru1, ru2, rv1, rv2, rwn, rwo, ra, ras, rl1, rl0, rf,
):
    ctx = lax.axis_index("ctx")
    shard = lax.axis_index("shard")
    y, x, z, c = ctx // 4, ctx % 4, shard // 2, shard % 2
    head_first = shard * HEADS

    def at(dy=0, dx=0, dz=0, dc=0):
        return (((y + dy) % 4) * 4 + (x + dx) % 4, ((z + dz) % 4) * 2 + (c + dc) % 2)

    barrier = pltpu.get_barrier_semaphore()
    for dy, dx, dz, dc in PEERS:
        pl.semaphore_signal(barrier, inc=1, device_id=at(dy, dx, dz, dc), device_id_type=MESH)

    pending = []
    counter = [0]

    def send(src, dst, recv, target, condition=None):
        k = counter[0]
        counter[0] += 1
        copy = pltpu.make_async_remote_copy(
            src_ref=src, dst_ref=dst, send_sem=ssem.at[k], recv_sem=recv,
            device_id=target, device_id_type=MESH,
        )
        copy.start()
        pending.append((src, k, condition))

    def arrived(ref, sem):
        pltpu.make_async_copy(ref, ref, sem).wait()

    for half in range(2):
        rows = []
        for k in range(4):
            h = half * 4 + k
            f = block_factor(
                [power(keys_scale[b, head_first + h]) for b in range(4)], (1, LATENT), 1, 0
            )
            rows.append(up_keys[h].astype(F32) * f)
        upk[half, pl.ds(y, 1), pl.ds(x, 1)] = jnp.concatenate(rows, axis=0).astype(BF16)[None, None]

    for h in range(HEADS):
        f = power(values_scale[y, head_first + h])
        upv[pl.ds(y, 1), pl.ds(x, 1), h * 32 : (h + 1) * 32, :] = (
            (up_values[h].astype(F32) * f).astype(BF16)[None, None]
        )

    chunk = [(y + 4 - i) % 4 for i in range(4)]
    features = [pl.ds(((z + d) % 4) * PIECE, PIECE) for d in range(4)]
    my_lanes = pl.ds(pl.multiple_of(c * 512, 512), 512)
    my_halves = [pl.ds(pl.multiple_of(c * 512 + k * 256, 256), 256) for k in range(2)]
    its_lanes = pl.ds(pl.multiple_of((1 - c) * 512, 512), 512)
    own_lanes = pl.ds(pl.multiple_of(c * 128, 128), 128)
    own_place = pl.ds(pl.multiple_of(c * 512 + x * 128, 128), 128)

    pl.semaphore_wait(barrier, len(PEERS))

    own_keys, own_slot = latent_keys.at[features[0], own_lanes], kbuf.at[y, features[0], own_place]
    for d in (1, 3, 2):
        send(own_keys, own_slot, rk1x, at(dx=d))
    pltpu.make_async_copy(own_keys, own_slot, rk1x).start()
    for d in (1, 3, 2):
        piece = upk.at[0, y, x]
        send(piece, piece, ru1.at[0, d], at(dy=d))

    def needed(i, action):
        if i == 0:
            action()
        else:
            pl.when(y >= i)(action)

    def keys_along_z(i):
        part = kbuf.at[chunk[i], features[0], my_lanes]
        condition = None if i == 0 else y >= i

        def action():
            if i > 0:
                arrived(part, rk1y.at[i])
            for d in (1, 3):
                send(part, part, rkz.at[i, d], at(dz=d), condition)
            send(part, part, rks.at[i], at(dc=1), condition)

        needed(i, action)

    def keys_relay(i):
        condition = None if i == 0 else y >= i

        def action():
            for d in (1, 3):
                part = kbuf.at[chunk[i], features[4 - d], my_lanes]
                arrived(part, rkz.at[i, d])
                half = kbuf.at[chunk[i], features[4 - d], my_halves[d // 2]]
                send(half, half, rkz.at[i, 2], at(dz=d), condition)
                send(part, part, rks.at[i], at(dc=1), condition)

        needed(i, action)

    def keys_far(i):
        condition = None if i == 0 else y >= i

        def action():
            part = kbuf.at[chunk[i], features[2], my_lanes]
            arrived(part, rkz.at[i, 2])
            send(part, part, rks.at[i], at(dc=1), condition)

        needed(i, action)

    def keys_ready(i):
        needed(i, lambda: arrived(kbuf.at[chunk[i], :, its_lanes], rks.at[i]))

    first_block = (ctx * 7) // 2
    shift = (ctx % 2) * 64
    for h in range(HEADS):
        f = block_factor(
            [power(out_scale[first_block + b, head_first + h]) for b in range(4)], (COLS, 1), 0, shift
        )
        wsend[:, h * VDIM : (h + 1) * VDIM] = (out_weight[h].astype(F32) * f).astype(BF16)

    arrived(kbuf.at[y, features[0], my_lanes], rk1x)
    keys_along_z(0)
    for d in (1, 2, 3):
        part = kbuf.at[y, features[0], my_lanes]
        condition = y + d < 4
        pl.when(condition)(lambda: send(part, part, rk1y.at[d], at(dy=d), condition))
    y_from = [(y + 4 - d) % 4 for d in range(4)]
    x_from = [(x + 4 - d) % 4 for d in range(4)]
    for d in (1, 3, 2):
        arrived(upk.at[0, y_from[d], x], ru1.at[0, d])
    for d in (1, 3, 2):
        send(upk.at[0, :, x], upk.at[0, :, x], ru2.at[0, d], at(dx=d))
    for d in (1, 3, 2):
        send(upk.at[1, y, x], upk.at[1, y, x], ru1.at[1, d], at(dy=d))
    for d in (1, 3, 2):
        send(upv.at[y, x], upv.at[y, x], rv1.at[d], at(dy=d))
    keys_relay(0)
    keys_along_z(1)
    for d in (1, 3, 2):
        arrived(upk.at[0, :, x_from[d]], ru2.at[0, d])

    owner = y // 2
    up_one, down_one = (((y + 1) % 4) * 4 + x, z * 2 + owner), (((y + 3) % 4) * 4 + x, z * 2 + owner)
    weight_lanes = pl.ds(pl.multiple_of(c * 1024, 1024), 1024)
    weight_rows = [pl.ds(0, COLS // 2), pl.ds(COLS // 2, COLS // 2)]
    for order in range(2):
        for half, target in ((order, up_one), (1 - order, down_one)):
            rows = weight_rows[half]
            send(wsend.at[rows], wbuf.at[y % 2, rows, weight_lanes], rwn.at[c, half], target)
    own_weight = owner == c

    @pl.when(own_weight)
    def _():
        pltpu.make_async_copy(wsend, wbuf.at[y % 2, :, weight_lanes], rwo.at[c]).start()

    sibling_weight = pltpu.make_async_remote_copy(
        src_ref=wsend, dst_ref=wbuf.at[y % 2, :, weight_lanes], send_sem=sw.at[0], recv_sem=rwo.at[c],
        device_id=at(dc=1), device_id_type=MESH,
    )

    @pl.when(jnp.logical_not(own_weight))
    def _():
        sibling_weight.start()

    near_slot = (y + 1) % 2
    from_below = (2 * c + near_slot + 4 - y) % 4 == 3

    def weight_relay():
        half = jnp.where(from_below, 0, 1)
        for k in range(2):
            arrived(wbuf.at[near_slot, weight_rows[0], pl.ds(0, 1024)], rwn.at[k, half])
        part = wbuf.at[near_slot, pl.ds(half * (COLS // 2), COLS // 2)]
        step = jnp.where(from_below, 1, 3)
        send(part, part, rwo.at[half], (((y + step) % 4) * 4 + x, shard))

    def weight_ready():
        rest = jnp.where(from_below, 1, 0)
        for k in range(2):
            arrived(wbuf.at[near_slot, weight_rows[0], pl.ds(0, 1024)], rwn.at[k, rest])
        for k in range(2):
            arrived(wbuf.at[y % 2, :, pl.ds(0, 1024)], rwo.at[k])

    def make_queries(half):
        tiles = upk[half].astype(F32).reshape(16, 4, 8, LATENT)
        for k in range(4):
            h = half * 4 + k
            weight = tiles[:, k].reshape(NOPE, LATENT).astype(BF16)
            content = queries[:, h * HEAD : h * HEAD + NOPE]
            latent = jnp.dot(content, weight, preferred_element_type=F32).astype(BF16)
            rotary = queries[:, h * HEAD + NOPE : (h + 1) * HEAD]
            for part in range(2):
                rows = slice(part * 1024 + h * 128, part * 1024 + (h + 1) * 128)
                tokens = slice(part * 128, (part + 1) * 128)
                qbuf[rows, :LATENT] = latent[tokens]
                qbuf[rows, LATENT:] = rotary[tokens]

    def chunk_of(i):
        return (y + 4 - i) % 4

    def attend(units, first=False):

        def score(i, part, group):
            first_row = part * 1024 + group * 512
            scores = jnp.dot(
                qbuf[first_row : first_row + 512, :], kbuf[chunk_of(i)], preferred_element_type=F32
            )
            if first:
                row = lax.broadcasted_iota(jnp.int32, (512, CHUNK), 0) % 128 + (x * TOKENS + part * 128)
                col = lax.broadcasted_iota(jnp.int32, (512, CHUNK), 1)
                place = ((col % 512) // 128) * TOKENS + (col // 512) * 128 + col % 128
                scores = jnp.where(place <= row, scores, -1e30)
            return scores

        def mix(scores, i, part, group):
            rows = slice(part * 1024 + group * 512, part * 1024 + group * 512 + 512)
            newest = jnp.max(scores, axis=1, keepdims=True)
            if not first:
                last = mx[rows, :1]
                newest = jnp.maximum(last, newest)
            weights = jnp.exp2((scores - newest) * FACTOR)
            total = jnp.sum(weights, axis=1, keepdims=True)
            mx[rows, :] = jnp.broadcast_to(newest, (512, 128))
            mixture = lax.dot_general(
                weights.astype(BF16), kbuf[chunk_of(i), :LATENT], (((1,), (1,)), ((), ())),
                preferred_element_type=F32,
            )
            if first:
                ls[rows, :] = jnp.broadcast_to(total, (512, 128))
                acc[rows, :] = mixture
            else:
                decay = jnp.exp2((last - newest) * FACTOR)
                ls[rows, :] = ls[rows, :] * decay + total
                acc[rows, :] = acc[rows, :] * decay + mixture

        scores = score(*units[0])
        for n, unit in enumerate(units):
            following = score(*units[n + 1]) if n + 1 < len(units) else None
            mix(scores, *unit)
            scores = following

    def value_lanes(core):
        return pl.ds(pl.multiple_of(core * 1024, 1024), 1024)

    def value_place(part, place, core):
        rows = pl.ds(pl.multiple_of((place % 2) * 128, 128), 128)
        return abuf.at[part * 2 + place // 2, rows, value_lanes(core)]

    def finish(part, group):
        for h in range(group * 4, group * 4 + 4):
            rows = slice(part * 1024 + h * 128, part * 1024 + (h + 1) * 128)
            head_latent = (acc[rows, :] / ls[rows, :1]).astype(BF16)
            tile = upv[:, :, h * 32 : (h + 1) * 32, :].reshape(LATENT, VDIM)
            value = jnp.dot(head_latent, tile, preferred_element_type=F32).astype(BF16)
            lanes = pl.ds(pl.multiple_of(c * 1024 + h * VDIM, VDIM), VDIM)
            abuf[part * 2 + x // 2, pl.ds(pl.multiple_of((x % 2) * 128, 128), 128), lanes] = value
        rows = pl.ds(pl.multiple_of((x % 2) * 128, 128), 128)
        lanes = pl.ds(pl.multiple_of(c * 1024 + group * 512, 512), 512)
        piece = abuf.at[part * 2 + x // 2, rows, lanes]
        for d in (1, 3):
            send(piece, piece, ra.at[part, d], at(dx=d))
        send(piece, piece, ras.at[part], at(dc=1))

    def values_relay(part):
        for d in (1, 3):
            piece = value_place(part, x_from[d], c)
            arrived(piece, ra.at[part, d])
            start = pl.multiple_of((x_from[d] % 2) * 128 + (d // 2) * 64, 64)
            half = abuf.at[part * 2 + x_from[d] // 2, pl.ds(start, 64), value_lanes(c)]
            send(half, half, ra.at[part, 2], at(dx=d))
            send(piece, piece, ras.at[part], at(dc=1))

    def values_far(part):
        piece = value_place(part, x_from[2], c)
        arrived(piece, ra.at[part, 2])
        send(piece, piece, ras.at[part], at(dc=1))

    def values_ready(part):
        arrived(abuf.at[pl.ds(part * 2, 2), :, value_lanes(1 - c)], ras.at[part])

    def rest_of_chunks(part, group):
        @pl.when(y == 3)
        def _():
            attend([(i, part, group) for i in (1, 2, 3)])

        @pl.when(y < 3)
        def _():
            def step(i, carry):
                attend([(i, part, group)])
                return carry

            lax.fori_loop(1, y + 1, step, 0)

    for d in (1, 3, 2):
        arrived(upk.at[1, y_from[d], x], ru1.at[1, d])
    for d in (1, 3, 2):
        send(upk.at[1, :, x], upk.at[1, :, x], ru2.at[1, d], at(dx=d))
    keys_far(0)
    keys_along_z(2)
    keys_along_z(3)
    make_queries(0)
    keys_ready(0)
    attend([(0, 0, 0), (0, 1, 0)], True)
    keys_relay(1)
    for d in (1, 3, 2):
        arrived(upk.at[1, :, x_from[d]], ru2.at[1, d])
    for d in (1, 3, 2):
        arrived(upv.at[y_from[d], x], rv1.at[d])
    for d in (1, 3, 2):
        send(upv.at[:, x], upv.at[:, x], rv2.at[d], at(dx=d))
    make_queries(1)
    attend([(0, 0, 1), (0, 1, 1)], True)
    keys_far(1)
    keys_relay(2)
    keys_relay(3)
    keys_ready(1)
    needed(1, lambda: attend([(1, 0, 0), (1, 0, 1)]))
    keys_far(2)
    keys_far(3)
    keys_ready(2)
    needed(2, lambda: attend([(2, 0, 0), (2, 0, 1)]))
    weight_relay()
    keys_ready(3)
    needed(3, lambda: attend([(3, 0, 0), (3, 0, 1)]))
    for d in (1, 3, 2):
        arrived(upv.at[:, x_from[d]], rv2.at[d])
    finish(0, 0)
    finish(0, 1)
    rest_of_chunks(1, 0)
    finish(1, 0)
    rest_of_chunks(1, 1)
    values_relay(0)
    finish(1, 1)
    values_far(0)
    weight_ready()
    values_ready(0)

    near = (z + 1) % 2
    other = z % 2
    is_own = z // 2 == c
    near_up = (2 * c + near + 4 - z) % 4 == 1
    near_half = jnp.where(near_up, 0, 1)
    z_near = jnp.where(near_up, 1, 3)

    def project(slot, t):
        part = lax.dot_general(
            wbuf[slot], abuf[t], (((1,), (1,)), ((), ())), preferred_element_type=F32
        )
        cbuf[slot, t] = part.astype(BF16)

    def far_copy(t, half):
        return pltpu.make_async_remote_copy(
            src_ref=cbuf.at[other, t, pl.ds(half * (COLS // 2), COLS // 2)], dst_ref=land1.at[t],
            send_sem=sc.at[t, half], recv_sem=rl1.at[t],
            device_id=at(dz=1 if half == 0 else 3), device_id_type=MESH,
        )

    def near_copy(t):
        return pltpu.make_async_remote_copy(
            src_ref=cbuf.at[near, t], dst_ref=land0.at[near_half, t],
            send_sem=sl.at[t], recv_sem=rl0.at[near_half, t],
            device_id=at(dz=z_near), device_id_type=MESH,
        )

    first = jnp.where(is_own, near, other)

    def first_step(t, carry):
        project(first, t)

        @pl.when(jnp.logical_not(is_own))
        def _():
            far_copy(t, 0).start()
            far_copy(t, 1).start()

        return carry

    def second_step(t, carry):
        project(1 - first, t)
        return carry

    def near_step(t, carry):
        arrived(land1.at[t], rl1.at[t])
        rows = pl.ds(near_half * (COLS // 2), COLS // 2)
        total = cbuf[near, t, rows].astype(F32) + land1[t].astype(F32)
        cbuf[near, t, rows] = total.astype(BF16)
        near_copy(t).start()
        return carry

    receiver = x // 2

    def final_copy(t, k):
        place = (t % 2) * 2 + k
        lanes = pl.ds(pl.multiple_of((t // 2) * 128, 128), 128)
        source, target = fin.at[t, :, k * 128 : (k + 1) * 128], outbuf.at[x % 2, :, lanes]
        here = jnp.logical_and(place == x, receiver == c)
        local = pltpu.make_async_copy(source, target, rf.at[x % 2])
        remote = pltpu.make_async_remote_copy(
            src_ref=source, dst_ref=target, send_sem=sa.at[t, k], recv_sem=rf.at[x % 2],
            device_id=(y * 4 + place, z * 2 + receiver), device_id_type=MESH,
        )
        return here, local, remote

    def final_step(t, carry):
        arrived(land0.at[0, t], rl0.at[0, t])
        arrived(land0.at[1, t], rl0.at[1, t])
        total = cbuf[other, t].astype(F32) + land0[0, t].astype(F32) + land0[1, t].astype(F32)
        fin[t] = total.astype(BF16)
        for k in range(2):
            here, local, remote = final_copy(t, k)
            pl.when(here)(local.start)
            pl.when(jnp.logical_not(here))(remote.start)
        return carry

    lax.fori_loop(0, 2, first_step, 0)
    lax.fori_loop(0, 2, second_step, 0)
    values_relay(1)
    lax.fori_loop(0, 2, near_step, 0)
    values_far(1)
    values_ready(1)
    lax.fori_loop(2, 4, first_step, 0)
    lax.fori_loop(2, 4, second_step, 0)

    @pl.when(is_own)
    def _():
        lax.fori_loop(0, 2, final_step, 0)

    lax.fori_loop(2, 4, near_step, 0)

    @pl.when(is_own)
    def _():
        lax.fori_loop(2, 4, final_step, 0)

    for k in range(2):
        arrived(outbuf.at[k], rf.at[k])
    out[:COLS, :] = outbuf[0]
    out[COLS:, :] = outbuf[1]

    for ref, k, condition in pending:
        if condition is None:
            arrived(ref, ssem.at[k])
        else:
            pl.when(condition)(functools.partial(lambda r, n: arrived(r, ssem.at[n]), ref, k))

    @pl.when(jnp.logical_not(own_weight))
    def _():
        sibling_weight.wait_send()

    def sent_near(t, carry):
        near_copy(t).wait_send()
        return carry

    def sent_far(t, carry):
        far_copy(t, 0).wait_send()
        far_copy(t, 1).wait_send()
        return carry

    def sent_final(t, carry):
        for k in range(2):
            here, local, remote = final_copy(t, k)
            pl.when(jnp.logical_not(here))(remote.wait_send)
        return carry

    lax.fori_loop(0, 4, sent_near, 0)

    @pl.when(jnp.logical_not(is_own))
    def _():
        lax.fori_loop(0, 4, sent_far, 0)

    @pl.when(is_own)
    def _():
        lax.fori_loop(0, 4, sent_final, 0)


def body(queries, latent_keys, up_keys, up_values, out_weight, keys_scale, values_scale, out_scale):
    vmem = pl.BlockSpec(memory_space=pltpu.VMEM)
    smem = pl.BlockSpec(memory_space=pltpu.SMEM)
    dma = pltpu.SemaphoreType.DMA
    result = pl.pallas_call(
        kernel,
        out_shape=jax.ShapeDtypeStruct((2 * COLS, TOKENS), BF16),
        in_specs=[vmem] * 5 + [smem] * 3,
        out_specs=vmem,
        scratch_shapes=[
            pltpu.VMEM((4, WIDE, CHUNK), BF16),
            pltpu.VMEM((2, 4, 4, 32, LATENT), BF16),
            pltpu.VMEM((4, 4, 256, VDIM), BF16),
            pltpu.VMEM((HEADS * TOKENS, WIDE), BF16),
            pltpu.VMEM((HEADS * TOKENS, LATENT), F32),
            pltpu.VMEM((HEADS * TOKENS, 128), F32),
            pltpu.VMEM((HEADS * TOKENS, 128), F32),
            pltpu.VMEM((2, COLS, 2048), BF16),
            pltpu.VMEM((COLS, 1024), BF16),
            pltpu.VMEM((4, TOKENS, 2048), BF16),
            pltpu.VMEM((2, 4, COLS, TOKENS), BF16),
            pltpu.VMEM((4, COLS // 2, TOKENS), BF16),
            pltpu.VMEM((2, 4, COLS, TOKENS), BF16),
            pltpu.VMEM((4, COLS, TOKENS), BF16),
            pltpu.VMEM((2, COLS, TOKENS), BF16),
            dma((128,)),
            dma((1,)),
            dma((4, 2)),
            dma((4, 2)),
            dma((4,)),
            dma,
            dma((4,)),
            dma((4, 4)),
            dma((4,)),
            dma((3, 4)),
            dma((3, 4)),
            dma((4,)),
            dma((4,)),
            dma((2, 2)),
            dma((2,)),
            dma((2, 4)),
            dma((2,)),
            dma((4,)),
            dma((2, 4)),
            dma((2,)),
        ],
        compiler_params=pltpu.CompilerParams(
            collective_id=0, has_side_effects=True, vmem_limit_bytes=56 * 2**20
        ),
        name="attention",
    )(
        queries, latent_keys.T, up_keys, up_values, out_weight.swapaxes(1, 2),
        keys_scale.T, values_scale.T, out_scale.T,
    )
    return result.T


def solution(mesh):
    return jax.shard_map(
        body,
        mesh=mesh,
        in_specs=(
            P("ctx", "shard"),
            P("ctx", None),
            P("shard", "ctx", None),
            P("shard", "ctx", None),
            P("shard", None, "ctx"),
            P(),
            P(),
            P(),
        ),
        out_specs=P("ctx", "shard"),
        check_vma=False,
    )
```

```python
import functools

import jax
import jax.numpy as jnp
from jax import lax
from jax.experimental import pallas as pl
from jax.experimental.pallas import tpu as pltpu
from jax.sharding import PartitionSpec as P

NOPE = 128
ROPE = 64
HEAD = NOPE + ROPE
LATENT = 512
WIDE = LATENT + ROPE
VDIM = 128
HEADS = 8
TOKENS = 256
CHUNK = 4 * TOKENS
COLS = 448
PIECE = WIDE // 4
MESH = pl.DeviceIdType.MESH
FACTOR = (NOPE + ROPE) ** (-0.5) * 1.4426950408889634
F32 = jnp.float32
BF16 = jnp.bfloat16

PEERS = (
    [(0, d, 0, k) for d in (1, 2, 3) for k in (0, 1)]
    + [(1, 0, 0, 0), (2, 0, 0, 0), (3, 0, 0, 0), (1, 0, 0, 1), (3, 0, 0, 1)]
    + [(0, 0, d, 0) for d in (1, 2, 3)]
    + [(0, 0, 0, 1)]
)


def power(exponent):
    return jnp.where(exponent > 0, 2.0, jnp.where(exponent < 0, 0.5, 1.0)).astype(F32)


def block_factor(values, shape, dim, shift):
    block = (lax.broadcasted_iota(jnp.int32, shape, dim) + shift) // 128
    result = jnp.full(shape, values[0], F32)
    for k in range(1, len(values)):
        result = jnp.where(block == k, values[k], result)
    return result


def kernel(
    queries, latent_keys, up_keys, up_values, out_weight, keys_scale, values_scale, out_scale,
    out,
    kbuf, upk, upv, qbuf, acc, mx, ls, wbuf, wsend, abuf, cbuf, land1, land0, fin, outbuf,
    ssem, sw, sa, sc, sl, rk1x, rk1y, rkz, rks, ru1, ru2, rv1, rv2, rwn, rwo, ra, ras, rl1, rl0, rf,
):
    ctx = lax.axis_index("ctx")
    shard = lax.axis_index("shard")
    y, x, z, c = ctx // 4, ctx % 4, shard // 2, shard % 2
    head_first = shard * HEADS

    def at(dy=0, dx=0, dz=0, dc=0):
        return (((y + dy) % 4) * 4 + (x + dx) % 4, ((z + dz) % 4) * 2 + (c + dc) % 2)

    barrier = pltpu.get_barrier_semaphore()
    for dy, dx, dz, dc in PEERS:
        pl.semaphore_signal(barrier, inc=1, device_id=at(dy, dx, dz, dc), device_id_type=MESH)

    pending = []
    counter = [0]

    def send(src, dst, recv, target, condition=None):
        k = counter[0]
        counter[0] += 1
        copy = pltpu.make_async_remote_copy(
            src_ref=src, dst_ref=dst, send_sem=ssem.at[k], recv_sem=recv,
            device_id=target, device_id_type=MESH,
        )
        copy.start()
        pending.append((src, k, condition))

    def arrived(ref, sem):
        pltpu.make_async_copy(ref, ref, sem).wait()

    for half in range(2):
        rows = []
        for k in range(4):
            h = half * 4 + k
            f = block_factor(
                [power(keys_scale[b, head_first + h]) for b in range(4)], (1, LATENT), 1, 0
            )
            rows.append(up_keys[h].astype(F32) * f)
        upk[half, pl.ds(y, 1), pl.ds(x, 1)] = jnp.concatenate(rows, axis=0).astype(BF16)[None, None]

    for h in range(HEADS):
        f = power(values_scale[y, head_first + h])
        upv[pl.ds(y, 1), pl.ds(x, 1), h * 32 : (h + 1) * 32, :] = (
            (up_values[h].astype(F32) * f).astype(BF16)[None, None]
        )

    chunk = [(y + 4 - i) % 4 for i in range(4)]
    features = [pl.ds(((z + d) % 4) * PIECE, PIECE) for d in range(4)]
    my_lanes = pl.ds(pl.multiple_of(c * 512, 512), 512)
    my_halves = [pl.ds(pl.multiple_of(c * 512 + k * 256, 256), 256) for k in range(2)]
    its_lanes = pl.ds(pl.multiple_of((1 - c) * 512, 512), 512)
    own_lanes = pl.ds(pl.multiple_of(c * 128, 128), 128)
    own_place = pl.ds(pl.multiple_of(c * 512 + x * 128, 128), 128)

    pl.semaphore_wait(barrier, len(PEERS))

    own_keys, own_slot = latent_keys.at[features[0], own_lanes], kbuf.at[y, features[0], own_place]
    for d in (1, 3, 2):
        send(own_keys, own_slot, rk1x, at(dx=d))
    pltpu.make_async_copy(own_keys, own_slot, rk1x).start()
    for d in (1, 3, 2):
        piece = upk.at[0, y, x]
        send(piece, piece, ru1.at[0, d], at(dy=d))

    def needed(i, action):
        if i == 0:
            action()
        else:
            pl.when(y >= i)(action)

    def keys_along_z(i):
        part = kbuf.at[chunk[i], features[0], my_lanes]
        condition = None if i == 0 else y >= i

        def action():
            if i > 0:
                arrived(part, rk1y.at[i])
            for d in (1, 3):
                send(part, part, rkz.at[i, d], at(dz=d), condition)
            send(part, part, rks.at[i], at(dc=1), condition)

        needed(i, action)

    def keys_relay(i):
        condition = None if i == 0 else y >= i

        def action():
            for d in (1, 3):
                part = kbuf.at[chunk[i], features[4 - d], my_lanes]
                arrived(part, rkz.at[i, d])
                half = kbuf.at[chunk[i], features[4 - d], my_halves[d // 2]]
                send(half, half, rkz.at[i, 2], at(dz=d), condition)
                send(part, part, rks.at[i], at(dc=1), condition)

        needed(i, action)

    def keys_far(i):
        condition = None if i == 0 else y >= i

        def action():
            part = kbuf.at[chunk[i], features[2], my_lanes]
            arrived(part, rkz.at[i, 2])
            send(part, part, rks.at[i], at(dc=1), condition)

        needed(i, action)

    def keys_ready(i):
        needed(i, lambda: arrived(kbuf.at[chunk[i], :, its_lanes], rks.at[i]))

    first_block = (ctx * 7) // 2
    shift = (ctx % 2) * 64
    for h in range(HEADS):
        f = block_factor(
            [power(out_scale[first_block + b, head_first + h]) for b in range(4)], (COLS, 1), 0, shift
        )
        wsend[:, h * VDIM : (h + 1) * VDIM] = (out_weight[h].astype(F32) * f).astype(BF16)

    arrived(kbuf.at[y, features[0], my_lanes], rk1x)
    keys_along_z(0)
    for d in (1, 2, 3):
        part = kbuf.at[y, features[0], my_lanes]
        condition = y + d < 4
        pl.when(condition)(lambda: send(part, part, rk1y.at[d], at(dy=d), condition))
    y_from = [(y + 4 - d) % 4 for d in range(4)]
    x_from = [(x + 4 - d) % 4 for d in range(4)]
    for d in (1, 3, 2):
        arrived(upk.at[0, y_from[d], x], ru1.at[0, d])
    for d in (1, 3, 2):
        send(upk.at[0, :, x], upk.at[0, :, x], ru2.at[0, d], at(dx=d))
    for d in (1, 3, 2):
        send(upk.at[1, y, x], upk.at[1, y, x], ru1.at[1, d], at(dy=d))
    for d in (1, 3, 2):
        send(upv.at[y, x], upv.at[y, x], rv1.at[d], at(dy=d))
    keys_relay(0)
    keys_along_z(1)
    for d in (1, 3, 2):
        arrived(upk.at[0, :, x_from[d]], ru2.at[0, d])

    owner = y // 2
    up_one, down_one = (((y + 1) % 4) * 4 + x, z * 2 + owner), (((y + 3) % 4) * 4 + x, z * 2 + owner)
    weight_lanes = pl.ds(pl.multiple_of(c * 1024, 1024), 1024)
    weight_rows = [pl.ds(0, COLS // 2), pl.ds(COLS // 2, COLS // 2)]
    for order in range(2):
        for half, target in ((order, up_one), (1 - order, down_one)):
            rows = weight_rows[half]
            send(wsend.at[rows], wbuf.at[y % 2, rows, weight_lanes], rwn.at[c, half], target)
    own_weight = owner == c

    @pl.when(own_weight)
    def _():
        pltpu.make_async_copy(wsend, wbuf.at[y % 2, :, weight_lanes], rwo.at[c]).start()

    sibling_weight = pltpu.make_async_remote_copy(
        src_ref=wsend, dst_ref=wbuf.at[y % 2, :, weight_lanes], send_sem=sw.at[0], recv_sem=rwo.at[c],
        device_id=at(dc=1), device_id_type=MESH,
    )

    @pl.when(jnp.logical_not(own_weight))
    def _():
        sibling_weight.start()

    near_slot = (y + 1) % 2
    from_below = (2 * c + near_slot + 4 - y) % 4 == 3

    def weight_relay():
        half = jnp.where(from_below, 0, 1)
        for k in range(2):
            arrived(wbuf.at[near_slot, weight_rows[0], pl.ds(0, 1024)], rwn.at[k, half])
        part = wbuf.at[near_slot, pl.ds(half * (COLS // 2), COLS // 2)]
        step = jnp.where(from_below, 1, 3)
        send(part, part, rwo.at[half], (((y + step) % 4) * 4 + x, shard))

    def weight_ready():
        rest = jnp.where(from_below, 1, 0)
        for k in range(2):
            arrived(wbuf.at[near_slot, weight_rows[0], pl.ds(0, 1024)], rwn.at[k, rest])
        for k in range(2):
            arrived(wbuf.at[y % 2, :, pl.ds(0, 1024)], rwo.at[k])

    def make_queries(half):
        tiles = upk[half].astype(F32).reshape(16, 4, 8, LATENT)
        for k in range(4):
            h = half * 4 + k
            weight = tiles[:, k].reshape(NOPE, LATENT).astype(BF16)
            content = queries[:, h * HEAD : h * HEAD + NOPE]
            latent = jnp.dot(content, weight, preferred_element_type=F32).astype(BF16)
            rotary = queries[:, h * HEAD + NOPE : (h + 1) * HEAD]
            for part in range(2):
                rows = slice(part * 1024 + h * 128, part * 1024 + (h + 1) * 128)
                tokens = slice(part * 128, (part + 1) * 128)
                qbuf[rows, :LATENT] = latent[tokens]
                qbuf[rows, LATENT:] = rotary[tokens]

    def chunk_of(i):
        return (y + 4 - i) % 4

    def attend(units, first=False):

        def score(i, part, group):
            first_row = part * 1024 + group * 512
            scores = jnp.dot(
                qbuf[first_row : first_row + 512, :], kbuf[chunk_of(i)], preferred_element_type=F32
            )
            if first:
                row = lax.broadcasted_iota(jnp.int32, (512, CHUNK), 0) % 128 + (x * TOKENS + part * 128)
                col = lax.broadcasted_iota(jnp.int32, (512, CHUNK), 1)
                place = ((col % 512) // 128) * TOKENS + (col // 512) * 128 + col % 128
                scores = jnp.where(place <= row, scores, -1e30)
            return scores

        def mix(scores, i, part, group):
            rows = slice(part * 1024 + group * 512, part * 1024 + group * 512 + 512)
            newest = jnp.max(scores, axis=1, keepdims=True)
            if not first:
                last = mx[rows, :1]
                newest = jnp.maximum(last, newest)
            weights = jnp.exp2((scores - newest) * FACTOR)
            total = jnp.sum(weights, axis=1, keepdims=True)
            mx[rows, :] = jnp.broadcast_to(newest, (512, 128))
            mixture = lax.dot_general(
                weights.astype(BF16), kbuf[chunk_of(i), :LATENT], (((1,), (1,)), ((), ())),
                preferred_element_type=F32,
            )
            if first:
                ls[rows, :] = jnp.broadcast_to(total, (512, 128))
                acc[rows, :] = mixture
            else:
                decay = jnp.exp2((last - newest) * FACTOR)
                ls[rows, :] = ls[rows, :] * decay + total
                acc[rows, :] = acc[rows, :] * decay + mixture

        scores = score(*units[0])
        for n, unit in enumerate(units):
            following = score(*units[n + 1]) if n + 1 < len(units) else None
            mix(scores, *unit)
            scores = following

    def value_lanes(core):
        return pl.ds(pl.multiple_of(core * 1024, 1024), 1024)

    def value_place(part, place, core):
        rows = pl.ds(pl.multiple_of((place % 2) * 128, 128), 128)
        return abuf.at[part * 2 + place // 2, rows, value_lanes(core)]

    def finish(part, group):
        for h in range(group * 4, group * 4 + 4):
            rows = slice(part * 1024 + h * 128, part * 1024 + (h + 1) * 128)
            head_latent = (acc[rows, :] / ls[rows, :1]).astype(BF16)
            tile = upv[:, :, h * 32 : (h + 1) * 32, :].reshape(LATENT, VDIM)
            value = jnp.dot(head_latent, tile, preferred_element_type=F32).astype(BF16)
            lanes = pl.ds(pl.multiple_of(c * 1024 + h * VDIM, VDIM), VDIM)
            abuf[part * 2 + x // 2, pl.ds(pl.multiple_of((x % 2) * 128, 128), 128), lanes] = value
        rows = pl.ds(pl.multiple_of((x % 2) * 128, 128), 128)
        lanes = pl.ds(pl.multiple_of(c * 1024 + group * 512, 512), 512)
        piece = abuf.at[part * 2 + x // 2, rows, lanes]
        for d in (1, 3):
            send(piece, piece, ra.at[part, d], at(dx=d))
        send(piece, piece, ras.at[part], at(dc=1))

    def values_relay(part):
        for d in (1, 3):
            piece = value_place(part, x_from[d], c)
            arrived(piece, ra.at[part, d])
            start = pl.multiple_of((x_from[d] % 2) * 128 + (d // 2) * 64, 64)
            half = abuf.at[part * 2 + x_from[d] // 2, pl.ds(start, 64), value_lanes(c)]
            send(half, half, ra.at[part, 2], at(dx=d))
            send(piece, piece, ras.at[part], at(dc=1))

    def values_far(part):
        piece = value_place(part, x_from[2], c)
        arrived(piece, ra.at[part, 2])
        send(piece, piece, ras.at[part], at(dc=1))

    def values_ready(part):
        arrived(abuf.at[pl.ds(part * 2, 2), :, value_lanes(1 - c)], ras.at[part])

    def rest_of_chunks(part, group):
        @pl.when(y == 3)
        def _():
            attend([(i, part, group) for i in (1, 2, 3)])

        @pl.when(y < 3)
        def _():
            def step(i, carry):
                attend([(i, part, group)])
                return carry

            lax.fori_loop(1, y + 1, step, 0)

    for d in (1, 3, 2):
        arrived(upk.at[1, y_from[d], x], ru1.at[1, d])
    for d in (1, 3, 2):
        send(upk.at[1, :, x], upk.at[1, :, x], ru2.at[1, d], at(dx=d))
    keys_far(0)
    keys_along_z(2)
    keys_along_z(3)
    make_queries(0)
    keys_ready(0)
    attend([(0, 0, 0), (0, 1, 0)], True)
    keys_relay(1)
    for d in (1, 3, 2):
        arrived(upk.at[1, :, x_from[d]], ru2.at[1, d])
    for d in (1, 3, 2):
        arrived(upv.at[y_from[d], x], rv1.at[d])
    for d in (1, 3, 2):
        send(upv.at[:, x], upv.at[:, x], rv2.at[d], at(dx=d))
    make_queries(1)
    attend([(0, 0, 1), (0, 1, 1)], True)
    keys_far(1)
    keys_relay(2)
    keys_relay(3)
    keys_ready(1)
    needed(1, lambda: attend([(1, 0, 0), (1, 0, 1)]))
    keys_far(2)
    keys_far(3)
    keys_ready(2)
    needed(2, lambda: attend([(2, 0, 0), (2, 0, 1)]))
    weight_relay()
    keys_ready(3)
    needed(3, lambda: attend([(3, 0, 0), (3, 0, 1)]))
    for d in (1, 3, 2):
        arrived(upv.at[:, x_from[d]], rv2.at[d])
    finish(0, 0)
    finish(0, 1)
    rest_of_chunks(1, 0)
    finish(1, 0)
    rest_of_chunks(1, 1)
    values_relay(0)
    finish(1, 1)
    values_far(0)
    weight_ready()
    values_ready(0)

    near = (z + 1) % 2
    other = z % 2
    is_own = z // 2 == c
    near_up = (2 * c + near + 4 - z) % 4 == 1
    near_half = jnp.where(near_up, 0, 1)
    z_near = jnp.where(near_up, 1, 3)

    def project(slot, t):
        part = lax.dot_general(
            wbuf[slot], abuf[t], (((1,), (1,)), ((), ())), preferred_element_type=F32
        )
        cbuf[slot, t] = part.astype(BF16)

    def far_copy(t, half):
        return pltpu.make_async_remote_copy(
            src_ref=cbuf.at[other, t, pl.ds(half * (COLS // 2), COLS // 2)], dst_ref=land1.at[t],
            send_sem=sc.at[t, half], recv_sem=rl1.at[t],
            device_id=at(dz=1 if half == 0 else 3), device_id_type=MESH,
        )

    def near_copy(t):
        return pltpu.make_async_remote_copy(
            src_ref=cbuf.at[near, t], dst_ref=land0.at[near_half, t],
            send_sem=sl.at[t], recv_sem=rl0.at[near_half, t],
            device_id=at(dz=z_near), device_id_type=MESH,
        )

    first = jnp.where(is_own, near, other)

    def first_step(t, carry):
        project(first, t)

        @pl.when(jnp.logical_not(is_own))
        def _():
            far_copy(t, 0).start()
            far_copy(t, 1).start()

        return carry

    def second_step(t, carry):
        project(1 - first, t)
        return carry

    def near_step(t, carry):
        arrived(land1.at[t], rl1.at[t])
        rows = pl.ds(near_half * (COLS // 2), COLS // 2)
        total = cbuf[near, t, rows].astype(F32) + land1[t].astype(F32)
        cbuf[near, t, rows] = total.astype(BF16)
        near_copy(t).start()
        return carry

    receiver = x // 2

    def final_copy(t, k):
        place = (t % 2) * 2 + k
        lanes = pl.ds(pl.multiple_of((t // 2) * 128, 128), 128)
        source, target = fin.at[t, :, k * 128 : (k + 1) * 128], outbuf.at[x % 2, :, lanes]
        here = jnp.logical_and(place == x, receiver == c)
        local = pltpu.make_async_copy(source, target, rf.at[x % 2])
        remote = pltpu.make_async_remote_copy(
            src_ref=source, dst_ref=target, send_sem=sa.at[t, k], recv_sem=rf.at[x % 2],
            device_id=(y * 4 + place, z * 2 + receiver), device_id_type=MESH,
        )
        return here, local, remote

    def final_step(t, carry):
        arrived(land0.at[0, t], rl0.at[0, t])
        arrived(land0.at[1, t], rl0.at[1, t])
        total = cbuf[other, t].astype(F32) + land0[0, t].astype(F32) + land0[1, t].astype(F32)
        fin[t] = total.astype(BF16)
        for k in range(2):
            here, local, remote = final_copy(t, k)
            pl.when(here)(local.start)
            pl.when(jnp.logical_not(here))(remote.start)
        return carry

    lax.fori_loop(0, 2, first_step, 0)
    lax.fori_loop(0, 2, second_step, 0)
    values_relay(1)
    values_far(1)
    lax.fori_loop(0, 2, near_step, 0)
    values_ready(1)
    lax.fori_loop(2, 4, first_step, 0)
    lax.fori_loop(2, 4, second_step, 0)

    @pl.when(is_own)
    def _():
        lax.fori_loop(0, 2, final_step, 0)

    lax.fori_loop(2, 4, near_step, 0)

    @pl.when(is_own)
    def _():
        lax.fori_loop(2, 4, final_step, 0)

    for k in range(2):
        arrived(outbuf.at[k], rf.at[k])
    out[:COLS, :] = outbuf[0]
    out[COLS:, :] = outbuf[1]

    for ref, k, condition in pending:
        if condition is None:
            arrived(ref, ssem.at[k])
        else:
            pl.when(condition)(functools.partial(lambda r, n: arrived(r, ssem.at[n]), ref, k))

    @pl.when(jnp.logical_not(own_weight))
    def _():
        sibling_weight.wait_send()

    def sent_near(t, carry):
        near_copy(t).wait_send()
        return carry

    def sent_far(t, carry):
        far_copy(t, 0).wait_send()
        far_copy(t, 1).wait_send()
        return carry

    def sent_final(t, carry):
        for k in range(2):
            here, local, remote = final_copy(t, k)
            pl.when(jnp.logical_not(here))(remote.wait_send)
        return carry

    lax.fori_loop(0, 4, sent_near, 0)

    @pl.when(jnp.logical_not(is_own))
    def _():
        lax.fori_loop(0, 4, sent_far, 0)

    @pl.when(is_own)
    def _():
        lax.fori_loop(0, 4, sent_final, 0)


def body(queries, latent_keys, up_keys, up_values, out_weight, keys_scale, values_scale, out_scale):
    vmem = pl.BlockSpec(memory_space=pltpu.VMEM)
    smem = pl.BlockSpec(memory_space=pltpu.SMEM)
    dma = pltpu.SemaphoreType.DMA
    result = pl.pallas_call(
        kernel,
        out_shape=jax.ShapeDtypeStruct((2 * COLS, TOKENS), BF16),
        in_specs=[vmem] * 5 + [smem] * 3,
        out_specs=vmem,
        scratch_shapes=[
            pltpu.VMEM((4, WIDE, CHUNK), BF16),
            pltpu.VMEM((2, 4, 4, 32, LATENT), BF16),
            pltpu.VMEM((4, 4, 256, VDIM), BF16),
            pltpu.VMEM((HEADS * TOKENS, WIDE), BF16),
            pltpu.VMEM((HEADS * TOKENS, LATENT), F32),
            pltpu.VMEM((HEADS * TOKENS, 128), F32),
            pltpu.VMEM((HEADS * TOKENS, 128), F32),
            pltpu.VMEM((2, COLS, 2048), BF16),
            pltpu.VMEM((COLS, 1024), BF16),
            pltpu.VMEM((4, TOKENS, 2048), BF16),
            pltpu.VMEM((2, 4, COLS, TOKENS), BF16),
            pltpu.VMEM((4, COLS // 2, TOKENS), BF16),
            pltpu.VMEM((2, 4, COLS, TOKENS), BF16),
            pltpu.VMEM((4, COLS, TOKENS), BF16),
            pltpu.VMEM((2, COLS, TOKENS), BF16),
            dma((128,)),
            dma((1,)),
            dma((4, 2)),
            dma((4, 2)),
            dma((4,)),
            dma,
            dma((4,)),
            dma((4, 4)),
            dma((4,)),
            dma((3, 4)),
            dma((3, 4)),
            dma((4,)),
            dma((4,)),
            dma((2, 2)),
            dma((2,)),
            dma((2, 4)),
            dma((2,)),
            dma((4,)),
            dma((2, 4)),
            dma((2,)),
        ],
        compiler_params=pltpu.CompilerParams(
            collective_id=0, has_side_effects=True, vmem_limit_bytes=56 * 2**20
        ),
        name="attention",
    )(
        queries, latent_keys.T, up_keys, up_values, out_weight.swapaxes(1, 2),
        keys_scale.T, values_scale.T, out_scale.T,
    )
    return result.T


def solution(mesh):
    return jax.shard_map(
        body,
        mesh=mesh,
        in_specs=(
            P("ctx", "shard"),
            P("ctx", None),
            P("shard", "ctx", None),
            P("shard", "ctx", None),
            P("shard", None, "ctx"),
            P(),
            P(),
            P(),
        ),
        out_specs=P("ctx", "shard"),
        check_vma=False,
    )
```
